32 devices in a mesh: tp: 2 (over x), dp: 16 (over z, y, core).
Axes of the slice: x: 2, y: 2, z: 4, core: 2. Of those that a mesh axis runs over, the one named last changes fastest.
Arguments:
- item_query: bfloat16 [2048, 2048], P('dp', 'tp'), may hold values from -20 to 20, as said below
- item_keys: bfloat16 [2048, 4, 2048], P('dp', None, 'tp'), may hold values from -20 to 20
- item_values: bfloat16 [2048, 4, 2048], P('dp', None, 'tp'), may hold values from -6 to 6
- item_out_weight: bfloat16 [2048, 4096], P('tp'), may hold values from -0.125 to 0.125
- item_residual: bfloat16 [2048, 4096], P('dp'), may hold values from -3 to 3
- cite_home: int32 [16384, 1], P('dp'), may hold values from 0 to 15; in each aligned block of 1024 rows (0 to 1023, 1024 to 2047, ...) at most 96 rows name the same one
- cite_row: int32 [16384], P('dp'), may hold values from 0 to 127
- seq_length: int32 [16], P('dp'), may hold values from 1 to 1024, 10240 in all
- user_gain: float32 [4096], replicated, may hold values from 0.1 to 1.9
- user_weight: bfloat16 [4096, 16, 384], P('dp', 'tp'), may hold values from -0.09375 to 0.09375
Outputs:
- user_qkv: bfloat16 [16384, 16, 384], P('dp', 'tp')
The draws below stay inside these ranges and needn't reach their ends.
Inputs may be any that keep to these rules, and one draw needn't show every extreme that they name: `item_query`: in hidden draws some items' queries equal a multiple of keys at their last two tokens. `cite_home`: among the 1024 positions of one sequence at most 96 cite items of one home device, and some home device is cited exactly 96 times. `seq_length`: some sequence has all 1024 positions live.
All inputs are finite; a program needn't handle non-finite values. No bound on the sum of `seq_length` on one device may be relied on, other than what follows from the above.
Results may differ from the reference program's by a relative error of at most 0.0065.
Values may be sent and summed in bfloat16 or wider, within the bound.
A program may use at most 128 MiB of HBM per device.

```python
import math
import jax
import jax.numpy as jnp
import numpy as np
from jax import lax

D = 4096
HEADS = 16
HEAD_DIM = 128
ITEMS_DEV = 128
ITEM_TOK = 4
USER_LEN = 1024
CAP = 96
ITEMS = 2048
ROWS = 16384
N_DP = 16


def paired_draw(key):
    base = jax.random.fold_in(key, 911)
    key_query, key_keys = jax.random.split(base, 2)
    queries = jnp.clip(jax.random.normal(key_query, (ITEMS, HEADS, HEAD_DIM), jnp.float32), -4.0, 4.0)
    keys_all = jnp.clip(jax.random.normal(key_keys, (ITEMS, ITEM_TOK, HEADS, HEAD_DIM), jnp.float32), -4.0, 4.0)
    return (queries, keys_all)


def draw_item_query(key, part):
    queries, keys_all = paired_draw(key)
    return queries.reshape(ITEMS, HEADS * HEAD_DIM).astype(jnp.bfloat16)


def draw_item_keys(key, part):
    queries, keys_all = paired_draw(key)
    return keys_all.reshape(ITEMS, ITEM_TOK, HEADS * HEAD_DIM).astype(jnp.bfloat16)


def set_ends(entries, own_key, smallest, high):
    spot = [jax.random.randint(jax.random.fold_in(own_key, axis), (), 0, length) for axis, length in enumerate(entries.shape)]
    longest = entries.shape.index(max(entries.shape))
    neighbour = spot[:longest] + [(spot[longest] + 1) % entries.shape[longest]] + spot[longest + 1:]
    return entries.at[tuple(spot)].set(smallest).at[tuple(neighbour)].set(high)


def steps_of(own_key, dims, shards, least, top_value):
    level, own = 1.0, jax.random.fold_in(own_key, 6)
    for axis_at, shards_of in shards:
        heights = jnp.exp(jax.random.uniform(jax.random.fold_in(own, axis_at), (shards_of,), jnp.float32, least / len(shards), top_value / len(shards)))
        level = level * jnp.repeat(heights, dims[axis_at] // shards_of).reshape([-1 if axis == axis_at else 1 for axis in range(len(dims))])
    return level


def length_profile(amount, total, reach, lean):
    portions = [(1 << 20) // math.isqrt(standing ** lean) + 1 for standing in range(2, amount + 1)]
    spare, given = total - reach - (amount - 1), [1] * (amount - 1)
    while spare > 0:
        free = [i for i in range(amount - 1) if given[i] < reach]
        mass, left = sum([portions[i] for i in free]), spare
        for i in free:
            more = min(reach - given[i], max(1, left * portions[i] // mass), spare)
            given[i] = given[i] + more
            spare = spare - more
    return np.array([reach] + given)


def ragged_sizes(rng, count, total, limit, skew):
    if count == 2:
        one = jax.random.randint(rng, (), max(1, total - limit), min(limit, total - 1) + 1)
        return jnp.stack([one, total - one])
    sizes = jnp.asarray(length_profile(count, total, limit, skew), jnp.int32)
    twos = (count - 1) // 2
    giver, receiver = sizes[1:1 + 2 * twos:2], sizes[2:2 + 2 * twos:2]
    room = jnp.minimum(giver - 1, limit - receiver)
    moved = jax.random.randint(jax.random.fold_in(rng, 1), (twos,), 0, 1 << 20) % (room + 1)
    sizes = sizes.at[1:1 + 2 * twos:2].set(giver - moved).at[2:2 + 2 * twos:2].set(receiver + moved)
    return sizes[jax.random.permutation(jax.random.fold_in(rng, 2), count)]


def deal_out(key, own, number, rows, count, top, most, skew):
    ranking = jax.random.permutation(key, count)
    heavy_load, ordinary = shares(count, rows * top, most, skew, True), shares(count, rows * top, most, skew, False)
    places = jnp.arange(count)

    def named(sizes, offset_by):
        used = int((sizes > 0).sum())
        fixed = max(1, used // 4)
        moved = fixed + (places - fixed + offset_by * (used - fixed)) % max(1, count - fixed)
        return jnp.zeros((count,), jnp.int32).at[ranking[jnp.where(places < fixed, places, moved)]].set(jnp.asarray(sizes, jnp.int32))

    sizes = jnp.where(number % 4 == 0, named(heavy_load, number // 4), named(ordinary, number - number // 4 - 1))
    mixed = jax.random.permutation(jax.random.fold_in(own, 3), count)
    source_of, taker = mixed[0:count // 2 * 2:2], mixed[1:count // 2 * 2:2]
    slack = jnp.minimum(sizes[source_of] - 1, most - sizes[taker]) // 2
    slack = jnp.where((source_of == ranking[0]) | (taker == ranking[0]) | (sizes[taker] == 0), 0, jnp.maximum(slack, 0))
    moved = jax.random.randint(jax.random.fold_in(own, 4), (count // 2,), 0, 1 << 20) % (slack + 1)
    sizes = sizes.at[source_of].add(-moved).at[taker].add(moved)
    members = jnp.searchsorted(jnp.cumsum(sizes), jnp.arange(rows * top), side="right").astype(jnp.int32)
    listing = members.reshape(top, rows).T
    listing = listing[jax.random.permutation(jax.random.fold_in(own, 1), rows)]
    offset_by = jax.random.randint(jax.random.fold_in(own, 2), (rows, 1), 0, top)
    return jnp.take_along_axis(listing, (jnp.arange(top)[None, :] + offset_by) % top, axis=1)


def shares(amount, total, limit, slope, full):
    loads = [(1 << 20) // math.isqrt(rank ** slope) + 1 for rank in range(1, amount + 1)]
    largest = limit if full else min(limit, max(-(-total // amount), total * loads[0] // sum(loads)))
    least = 1 if total - largest >= amount - 1 else 0
    given, spare = [largest] + [least] * (amount - 1), total - largest - least * (amount - 1)
    while spare > 0:
        free = [i for i in range(1, amount) if given[i] < largest] or [i for i in range(1, amount) if given[i] < limit]
        mass, remaining = sum([loads[i] for i in free]), spare
        for i in free:
            extra = min(limit - given[i], max(1, remaining * loads[i] // mass), spare)
            given[i] = given[i] + extra
            spare = spare - extra
    return np.array(given)


def normal_values(key, shape, spread, reach, cuts=(), held_as=jnp.bfloat16):
    values = spread * jax.random.normal(key, shape, jnp.float32)
    if cuts:
        values = values * steps_of(key, shape, cuts, -0.22, 0.18)
    return jnp.clip(values, -reach, reach).astype(held_as)


def setup_inputs(seed: int = 0) -> dict:
    streams_of = jax.random.split(jax.random.key(seed), 11)
    item_query = draw_item_query(jax.random.fold_in(streams_of[10], 71), 0)
    item_keys = draw_item_keys(jax.random.fold_in(streams_of[10], 71), 0)
    item_values = normal_values(streams_of[2], (ITEMS, ITEM_TOK, HEADS * HEAD_DIM), 1.0, 6.0, ((0, 16), (2, 2)))
    item_out_weight = normal_values(streams_of[3], (HEADS * HEAD_DIM, D), (HEADS * HEAD_DIM) ** -0.5, 0.125, ((0, 2),))
    item_residual = normal_values(streams_of[4], (ITEMS, D), 0.5, 3.0, ((0, 16),))
    cite_home_keys = jax.random.split(jax.random.fold_in(streams_of[5], 1), ROWS // USER_LEN)
    cite_home_turns = jax.random.permutation(jax.random.fold_in(streams_of[5], 3), ROWS // USER_LEN)
    cite_home = jax.vmap(lambda own, number: deal_out(jax.random.fold_in(streams_of[5], 2), own, number, USER_LEN, N_DP, 1, CAP, 2))(cite_home_keys, cite_home_turns).reshape((ROWS, 1))
    cite_row = set_ends(jax.random.randint(streams_of[6], (ROWS,), 0, ITEMS_DEV), jax.random.fold_in(streams_of[6], 1), 0, ITEMS_DEV - 1).astype(jnp.int32)
    seq_length = ragged_sizes(streams_of[7], N_DP, N_DP * USER_LEN * 5 // 8, USER_LEN, 2).astype(jnp.int32)
    user_gain = jnp.clip(1.0 + 0.18 * jax.random.normal(streams_of[8], (D,), jnp.float32), 0.1, 1.9)
    user_weight = normal_values(streams_of[9], (D, HEADS, 3 * HEAD_DIM), D ** -0.5, 0.09375, ((0, 16), (1, 2)))
    return dict(item_query=item_query, item_keys=item_keys, item_values=item_values, item_out_weight=item_out_weight, item_residual=item_residual, cite_home=cite_home, cite_row=cite_row, seq_length=seq_length, user_gain=user_gain, user_weight=user_weight)


def item_block(block):
    queries, keys_all, values_all = block
    count = queries.shape[0]
    queries = queries.astype(jnp.float32).reshape(count, HEADS, HEAD_DIM)
    keys_all = keys_all.astype(jnp.float32).reshape(count, ITEM_TOK, HEADS, HEAD_DIM)
    values_all = values_all.astype(jnp.float32).reshape(count, ITEM_TOK, HEADS, HEAD_DIM)
    scores = jnp.einsum('ihd,ithd->iht', queries, keys_all, precision=lax.Precision.HIGHEST) * (1.0 / math.sqrt(HEAD_DIM))
    probs = jax.nn.softmax(scores, axis=-1).astype(jnp.bfloat16).astype(jnp.float32)
    attended = jnp.einsum('iht,ithd->ihd', probs, values_all, precision=lax.Precision.HIGHEST)
    return attended.astype(jnp.bfloat16).reshape(count, HEADS * HEAD_DIM)

def reference(item_query, item_keys, item_values, item_out_weight, item_residual, cite_home, cite_row, seq_length, user_gain, user_weight):
    blocks = (item_query.reshape(N_DP, ITEMS_DEV, HEADS * HEAD_DIM), item_keys.reshape(N_DP, ITEMS_DEV, ITEM_TOK, HEADS * HEAD_DIM), item_values.reshape(N_DP, ITEMS_DEV, ITEM_TOK, HEADS * HEAD_DIM))
    attended = lax.map(item_block, blocks).reshape(N_DP * ITEMS_DEV, HEADS * HEAD_DIM)
    mixed = jnp.dot(attended, item_out_weight, preferred_element_type=jnp.float32)
    item_vec = (mixed + item_residual.astype(jnp.float32)).astype(jnp.bfloat16)
    index = (cite_home[:, 0] * ITEMS_DEV + cite_row).astype(jnp.int32)
    cited = jnp.take(item_vec, index, axis=0).reshape(N_DP, USER_LEN, D)
    weight_flat = user_weight.reshape(D, HEADS * 3 * HEAD_DIM)

    def owner(pair):
        rows, length = pair
        values32 = rows.astype(jnp.float32)
        scale = lax.rsqrt(lax.optimization_barrier(jnp.mean(values32 * values32, axis=1, keepdims=True)) + 1e-05)
        normed = (values32 * scale * user_gain[None, :]).astype(jnp.bfloat16)
        projected = jnp.dot(normed, weight_flat, preferred_element_type=jnp.float32)
        live = jnp.arange(USER_LEN, dtype=jnp.int32) < length
        return jnp.where(live[:, None], projected, jnp.zeros_like(projected)).astype(jnp.bfloat16)
    result = lax.map(owner, (cited, seq_length))
    return result.reshape(N_DP * USER_LEN, HEADS, 3 * HEAD_DIM)
```

```python
import math

import jax
import jax.numpy as jnp
from jax import lax
from jax.sharding import PartitionSpec as P

HEAD_DIM = 128


def attend(item_query, item_keys, item_values):
    count_items, width_heads = item_query.shape
    tokens_item = item_keys.shape[1]
    local_heads = width_heads // HEAD_DIM
    queries = item_query.reshape(count_items, local_heads, HEAD_DIM)
    keys_all = item_keys.reshape(count_items, tokens_item, local_heads, HEAD_DIM)
    values_all = item_values.reshape(count_items, tokens_item, local_heads, HEAD_DIM)
    scores = jnp.einsum("ihd,ithd->iht", queries, keys_all, preferred_element_type=jnp.float32) * (
        1.0 / math.sqrt(HEAD_DIM)
    )
    probs = jax.nn.softmax(scores, axis=-1).astype(jnp.bfloat16)
    attended = jnp.einsum("iht,ithd->ihd", probs, values_all, preferred_element_type=jnp.float32)
    return attended.astype(jnp.bfloat16).reshape(count_items, width_heads)


def per_device(
    item_query,
    item_keys,
    item_values,
    item_out_weight,
    item_residual,
    cite_home,
    cite_row,
    seq_length,
    user_gain,
    user_weight,
):
    devices, halves = lax.axis_size("dp"), lax.axis_size("tp")
    count_items = item_query.shape[0]
    shard_rows, user_heads, triple = user_weight.shape
    groups = devices // user_heads
    by_head = jnp.repeat(jnp.swapaxes(user_weight, 0, 1), groups, axis=0)
    weight = lax.all_to_all(by_head, "dp", split_axis=0, concat_axis=0, tiled=True)
    weight = weight.reshape(devices * shard_rows, triple)

    attended = attend(item_query, item_keys, item_values)
    partial_value = jnp.dot(attended, item_out_weight, preferred_element_type=jnp.float32)
    summed = lax.psum_scatter(partial_value, "tp", scatter_dimension=0, tiled=True)
    rows_half = count_items // halves
    mine = lax.dynamic_slice_in_dim(item_residual, lax.axis_index("tp") * rows_half, rows_half, 0)
    values32 = (summed + mine.astype(jnp.float32)).astype(jnp.bfloat16).astype(jnp.float32)
    scale = lax.rsqrt(jnp.mean(values32 * values32, axis=1, keepdims=True) + 1e-05)
    normed = (values32 * scale * user_gain[None, :]).astype(jnp.bfloat16)
    normed = lax.all_gather(normed, "tp", axis=0, tiled=True)
    members = [[part + groups * j for j in range(user_heads)] for part in range(groups)]
    normed = lax.all_gather(normed, "dp", axis_index_groups=members, axis=0, tiled=True)
    projected = jnp.dot(normed, weight, preferred_element_type=jnp.float32).astype(jnp.bfloat16)
    table = lax.all_gather(projected, "dp", axis=0, tiled=True)
    table = table.reshape(user_heads, devices * count_items, triple)

    home = cite_home[:, 0]
    place = (home % groups) * (user_heads * count_items) + (home // groups) * count_items + cite_row
    live = jnp.arange(home.shape[0], dtype=jnp.int32) < seq_length[0]
    place = jnp.where(live, place, -1)
    chosen = (place[:, None] == jnp.arange(devices * count_items, dtype=jnp.int32)[None, :]).astype(jnp.bfloat16)
    return jnp.einsum("rn,hnc->rhc", chosen, table, preferred_element_type=jnp.float32).astype(jnp.bfloat16)


def solution(mesh):
    in_specs = (
        P("dp", "tp"),
        P("dp", None, "tp"),
        P("dp", None, "tp"),
        P("tp", None),
        P("dp", None),
        P("dp", None),
        P("dp"),
        P("dp"),
        P(),
        P("dp", "tp", None),
    )
    out_specs = P("dp", "tp", None)
    return jax.shard_map(
        per_device, mesh=mesh, in_specs=in_specs, out_specs=out_specs, check_vma=False
    )
```

```python
import functools
import math

import jax
import jax.numpy as jnp
from jax import lax
from jax.experimental import pallas as pl
from jax.experimental.pallas import tpu as pltpu
from jax.sharding import PartitionSpec as P

HEAD_DIM = 128
CORES = 2
PARTS = 4
EPS = 1e-05
MESH = pl.DeviceIdType.MESH


def attend(item_query, item_keys, item_values):
    count_items, width_heads = item_query.shape
    tokens_item = item_keys.shape[1]
    local_heads = width_heads // HEAD_DIM
    queries = item_query.reshape(count_items, local_heads, HEAD_DIM)
    keys_all = item_keys.reshape(count_items, tokens_item, local_heads, HEAD_DIM)
    values_all = item_values.reshape(count_items, tokens_item, local_heads, HEAD_DIM)
    scores = jnp.einsum("ihd,ithd->iht", queries, keys_all, preferred_element_type=jnp.float32) * (
        1.0 / math.sqrt(HEAD_DIM)
    )
    probs = jax.nn.softmax(scores, axis=-1).astype(jnp.bfloat16)
    attended = jnp.einsum("iht,ithd->ihd", probs, values_all, preferred_element_type=jnp.float32)
    return attended.astype(jnp.bfloat16).reshape(count_items, width_heads)


class Grid:
    def __init__(self, devices, halves, heads):
        self.halves = halves
        self.near = halves
        self.far = devices // (CORES * self.near)
        self.splits = math.gcd(self.far, heads)
        self.share = self.far // self.splits
        self.blocks = devices

    def here(self):
        index = lax.axis_index("dp")
        return index // (self.near * CORES), (index // CORES) % self.near, index % CORES

    def at(self, far, near, core):
        return (far * self.near + near) * CORES + core


def greet(grid, with_halves):
    far, near, core = grid.here()
    barrier = pltpu.get_barrier_semaphore()
    count = 0
    peers = [{"dp": grid.at((far + k) % grid.far, near, core)} for k in range(1, grid.far)]
    peers += [{"dp": grid.at(far, (near + k) % grid.near, core)} for k in range(1, grid.near)]
    peers += [{"dp": grid.at(far, near, 1 - core)}]
    if with_halves:
        half = lax.axis_index("tp")
        peers += [{"tp": (half + k) % grid.halves} for k in range(1, grid.halves)]
    for peer in peers:
        pl.semaphore_signal(barrier, inc=1, device_id=peer, device_id_type=MESH)
        count += 1
    pl.semaphore_wait(barrier, count)


class Spread:
    def __init__(self, grid, source_for, out_ref, send_sem, recv_sem, own_sem):
        self.grid, self.source_for, self.out = grid, source_for, out_ref
        self.send_sem, self.recv_sem, self.own_sem = send_sem, recv_sem, own_sem
        self.rows = out_ref.shape[1] // PARTS
        self.sent, self.count = [], [0] * PARTS

    def send(self, part, source, block, peer):
        slot = self.count[part]
        self.count[part] += 1
        copy = pltpu.make_async_remote_copy(
            src_ref=source.at[pl.ds(part * self.rows, self.rows)],
            dst_ref=self.out.at[block, pl.ds(part * self.rows, self.rows)],
            send_sem=self.send_sem.at[part, slot],
            recv_sem=self.recv_sem.at[part, block],
            device_id={"dp": peer},
            device_id_type=MESH,
        )
        copy.start()
        self.sent.append(copy)

    def arrived(self, part, block):
        view = self.out.at[block, pl.ds(part * self.rows, self.rows)]
        pltpu.make_async_copy(view, view, self.recv_sem.at[part, block]).wait()

    def onward(self, part, source, block, near_too):
        grid = self.grid
        far, near, core = grid.here()
        if near_too:
            for k in range(1, grid.near):
                self.send(part, source, block, grid.at(far, (near + k) % grid.near, core))
        self.send(part, source, block, grid.at(far, near, 1 - core))

    def first(self, part):
        grid = self.grid
        far, near, core = grid.here()
        mine = grid.at(far, near, core)
        for k in range(1, grid.far):
            to = (far + k) % grid.far
            self.send(part, self.source_for(to), mine, grid.at(to, near, core))
        if part == 0:
            self.own = pltpu.make_async_copy(self.source_for(far), self.out.at[mine], self.own_sem)
            self.own.start()

    def second(self, part):
        grid = self.grid
        far, near, core = grid.here()
        self.onward(part, self.source_for(far), grid.at(far, near, core), True)
        for k in range(1, grid.far):
            block = grid.at((far + grid.far - k) % grid.far, near, core)
            self.arrived(part, block)
            self.onward(part, self.out.at[block], block, True)

    def third(self, part):
        grid = self.grid
        far, near, core = grid.here()
        for k in range(1, grid.near):
            for j in range(grid.far):
                block = grid.at((far + grid.far - j) % grid.far, (near + grid.near - k) % grid.near, core)
                self.arrived(part, block)
                self.onward(part, self.out.at[block], block, False)

    def last(self):
        grid = self.grid
        far, near, core = grid.here()
        for part in range(PARTS):
            for j in range(grid.far):
                for k in range(grid.near):
                    self.arrived(part, grid.at((far + j) % grid.far, (near + k) % grid.near, 1 - core))
        for copy in self.sent:
            copy.wait_send()
        self.own.wait()

    def run(self):
        for step in range(PARTS + 2):
            if step < PARTS:
                self.first(step)
            if 1 <= step <= PARTS:
                self.second(step - 1)
            if 2 <= step:
                self.third(step - 2)
        self.last()


def share_kernel(grid, block_ref, out_ref, send_sem, recv_sem, own_sem):
    greet(grid, False)
    Spread(grid, lambda to: block_ref, out_ref, send_sem, recv_sem, own_sem).run()


def items_kernel(
    grid, send_ref, base_ref, gain_ref, weight_ref, items_out, weight_out,
    partial_buf, mine_buf, half_send, half_recv, item_send, item_recv, item_own,
    send_sem, recv_sem, own_sem,
):
    far, near, core = grid.here()
    half = lax.axis_index("tp")
    greet(grid, True)
    halves = []
    for k in range(1, grid.halves):
        peer = (half + k) % grid.halves
        copy = pltpu.make_async_remote_copy(
            src_ref=send_ref.at[peer],
            dst_ref=partial_buf.at[k - 1],
            send_sem=half_send.at[k - 1],
            recv_sem=half_recv.at[k - 1],
            device_id={"tp": peer},
            device_id_type=MESH,
        )
        copy.start()
        halves.append(copy)
    spread = Spread(grid, lambda to: weight_ref.at[to // grid.share], weight_out, send_sem, recv_sem, own_sem)
    for part in range(PARTS):
        spread.first(part)
    for copy in halves:
        copy.wait()

    step_rows = 16

    def norm(i, carry):
        rows = pl.ds(pl.multiple_of(i * step_rows, step_rows), step_rows)
        total = base_ref[rows, :]
        for k in range(1, grid.halves):
            total = total + partial_buf[k - 1, rows, :].astype(jnp.float32)
        vec = total.astype(jnp.bfloat16).astype(jnp.float32)
        scale = lax.rsqrt(jnp.mean(vec * vec, axis=1, keepdims=True) + EPS)
        mine_buf[rows, :] = (vec * scale * gain_ref[...]).astype(jnp.bfloat16)
        return carry

    lax.fori_loop(0, mine_buf.shape[0] // step_rows, norm, 0)

    column, rest = far // grid.share, far % grid.share
    sent = []

    def send_items(source, place, slot, peer):
        copy = pltpu.make_async_remote_copy(
            src_ref=source,
            dst_ref=items_out.at[place, half],
            send_sem=item_send.at[slot],
            recv_sem=item_recv.at[place, half],
            device_id=peer,
            device_id_type=MESH,
        )
        copy.start()
        sent.append(copy)

    def arrived(place, part):
        view = items_out.at[place, part]
        pltpu.make_async_copy(view, view, item_recv.at[place, part]).wait()

    slot = 0
    for k in range(1, grid.splits):
        to = ((column + k) % grid.splits) * grid.share + rest
        send_items(mine_buf, column, slot, {"dp": grid.at(to, near, core)})
        slot += 1
    own = pltpu.make_async_copy(mine_buf, items_out.at[column, half], item_own)
    own.start()
    for k in range(1, grid.halves):
        send_items(mine_buf, column, slot, {"tp": (half + k) % grid.halves})
        slot += 1
    for part in range(PARTS):
        spread.second(part)
    for j in range(1, grid.splits):
        place = (column + grid.splits - j) % grid.splits
        arrived(place, half)
        for k in range(1, grid.halves):
            send_items(items_out.at[place, half], place, slot, {"tp": (half + k) % grid.halves})
            slot += 1
    for part in range(PARTS):
        spread.third(part)
    for k in range(1, grid.halves):
        for j in range(grid.splits):
            arrived((column + j) % grid.splits, (half + k) % grid.halves)
    for copy in sent:
        copy.wait_send()
    own.wait()
    spread.last()


def spread_sems(grid):
    sends = grid.far - 1 + grid.far * (grid.near - 1) + grid.far * grid.near
    return [
        pltpu.SemaphoreType.DMA((PARTS, sends)),
        pltpu.SemaphoreType.DMA((PARTS, grid.blocks)),
        pltpu.SemaphoreType.DMA,
    ]


def per_device(
    item_query,
    item_keys,
    item_values,
    item_out_weight,
    item_residual,
    cite_home,
    cite_row,
    seq_length,
    user_gain,
    user_weight,
):
    devices, halves = lax.axis_size("dp"), lax.axis_size("tp")
    count_items = item_query.shape[0]
    shard_rows, user_heads, triple = user_weight.shape
    grid = Grid(devices, halves, user_heads)
    splits, share, near, far = grid.splits, grid.share, grid.near, grid.far
    columns = user_heads * triple // splits
    width = item_residual.shape[1]
    rows_half = count_items // halves
    half = lax.axis_index("tp")
    any_space = pl.BlockSpec(memory_space=pl.ANY)
    in_vmem = pl.BlockSpec(memory_space=pltpu.VMEM)

    by_column = jnp.swapaxes(user_weight.reshape(shard_rows, splits, columns), 0, 1)
    attended = attend(item_query, item_keys, item_values)
    partial_value = jnp.dot(attended, item_out_weight, preferred_element_type=jnp.float32)
    to_send = partial_value.astype(jnp.bfloat16).reshape(halves, rows_half, width)
    base = lax.dynamic_slice_in_dim(partial_value, half * rows_half, rows_half, 0) + lax.dynamic_slice_in_dim(
        item_residual, half * rows_half, rows_half, 0
    ).astype(jnp.float32)
    sends = splits - 1 + splits * (halves - 1)
    normed, weight = pl.pallas_call(
        functools.partial(items_kernel, grid),
        out_shape=(
            jax.ShapeDtypeStruct((splits, halves, rows_half, width), jnp.bfloat16),
            jax.ShapeDtypeStruct((devices, shard_rows, columns), jnp.bfloat16),
        ),
        in_specs=[any_space, in_vmem, in_vmem, any_space],
        out_specs=(any_space, any_space),
        scratch_shapes=[
            pltpu.VMEM((halves - 1, rows_half, width), jnp.bfloat16),
            pltpu.VMEM((rows_half, width), jnp.bfloat16),
            pltpu.SemaphoreType.DMA((halves - 1,)),
            pltpu.SemaphoreType.DMA((halves - 1,)),
            pltpu.SemaphoreType.DMA((sends,)),
            pltpu.SemaphoreType.DMA((splits, halves)),
            pltpu.SemaphoreType.DMA,
        ]
        + spread_sems(grid),
        compiler_params=pltpu.CompilerParams(
            collective_id=0, has_side_effects=True, vmem_limit_bytes=24 << 20
        ),
        name="gather_items",
    )(to_send, base, user_gain[None, :], by_column)

    normed = normed.reshape(splits * count_items, width)
    weight = weight.reshape(devices * shard_rows, columns)
    projected = jnp.dot(normed, weight, preferred_element_type=jnp.float32).astype(jnp.bfloat16)
    table = pl.pallas_call(
        functools.partial(share_kernel, grid),
        out_shape=jax.ShapeDtypeStruct((devices,) + projected.shape, jnp.bfloat16),
        in_specs=[any_space],
        out_specs=any_space,
        scratch_shapes=spread_sems(grid),
        compiler_params=pltpu.CompilerParams(collective_id=1, has_side_effects=True),
        name="gather_table",
    )(projected)
    table = table.reshape(splits, devices * count_items, columns)

    home = cite_home[:, 0]
    home_far, home_near, home_core = home // (near * CORES), (home // CORES) % near, home % CORES
    block = ((home_far % share) * near + home_near) * CORES + home_core
    place = (block * splits + home_far // share) * count_items + cite_row
    live = jnp.arange(home.shape[0], dtype=jnp.int32) < seq_length[0]
    place = jnp.where(live, place, -1)
    chosen = (place[:, None] == jnp.arange(devices * count_items, dtype=jnp.int32)[None, :]).astype(jnp.bfloat16)
    out = jnp.einsum("rn,snc->rsc", chosen, table, preferred_element_type=jnp.float32).astype(jnp.bfloat16)
    return out.reshape(home.shape[0], user_heads, triple)


def solution(mesh):
    in_specs = (
        P("dp", "tp"),
        P("dp", None, "tp"),
        P("dp", None, "tp"),
        P("tp", None),
        P("dp", None),
        P("dp", None),
        P("dp"),
        P("dp"),
        P(),
        P("dp", "tp", None),
    )
    out_specs = P("dp", "tp", None)
    return jax.shard_map(
        per_device, mesh=mesh, in_specs=in_specs, out_specs=out_specs, check_vma=False
    )
```

```python
import functools
import math

import jax
import jax.numpy as jnp
from jax import lax
from jax.experimental import pallas as pl
from jax.experimental.pallas import tpu as pltpu
from jax.sharding import PartitionSpec as P

HEAD_DIM = 128
CORES = 2
TABLE_PARTS = 8
WEIGHT_PARTS = 4
ITEM_ROWS = 16
EPS = 1e-05
MESH = pl.DeviceIdType.MESH


def attend(item_query, item_keys, item_values):
    count_items, width_heads = item_query.shape
    tokens_item = item_keys.shape[1]
    local_heads = width_heads // HEAD_DIM
    queries = item_query.reshape(count_items, local_heads, HEAD_DIM)
    keys_all = item_keys.reshape(count_items, tokens_item, local_heads, HEAD_DIM)
    values_all = item_values.reshape(count_items, tokens_item, local_heads, HEAD_DIM)
    scores = jnp.einsum("ihd,ithd->iht", queries, keys_all, preferred_element_type=jnp.float32) * (
        1.0 / math.sqrt(HEAD_DIM)
    )
    probs = jax.nn.softmax(scores, axis=-1).astype(jnp.bfloat16)
    attended = jnp.einsum("iht,ithd->ihd", probs, values_all, preferred_element_type=jnp.float32)
    return attended.astype(jnp.bfloat16).reshape(count_items, width_heads)


class Grid:
    def __init__(self, devices, halves, heads):
        self.halves = halves
        self.near = halves
        self.far = devices // (CORES * self.near)
        self.splits = math.gcd(self.far, heads)
        self.share = self.far // self.splits
        self.blocks = devices

    def here(self):
        index = lax.axis_index("dp")
        return index // (self.near * CORES), (index // CORES) % self.near, index % CORES

    def at(self, far, near, core):
        return (far * self.near + near) * CORES + core


def nearest(place, count):
    order = [sorted(range(count), key=lambda other: (abs(other - at), other))[1:] for at in range(count)]
    found = []
    for k in range(count - 1):
        other = order[0][k]
        for at in range(1, count):
            other = jnp.where(place == at, order[at][k], other)
        found.append(other)
    return found


def beyond(place, origin, count):
    up = origin < place
    to = jnp.where(up, place + 1, place - 1)
    ok = jnp.logical_and(to >= 0, to < count)
    return jnp.clip(to, 0, count - 1), ok


def greet(grid, with_halves):
    far, near, core = grid.here()
    barrier = pltpu.get_barrier_semaphore()
    count = 0
    peers = [{"dp": grid.at((far + k) % grid.far, near, core)} for k in range(1, grid.far)]
    peers += [{"dp": grid.at(far, (near + k) % grid.near, core)} for k in range(1, grid.near)]
    peers += [{"dp": grid.at(far, near, 1 - core)}]
    if with_halves:
        half = lax.axis_index("tp")
        peers += [{"tp": (half + k) % grid.halves} for k in range(1, grid.halves)]
    for peer in peers:
        pl.semaphore_signal(barrier, inc=1, device_id=peer, device_id_type=MESH)
        count += 1
    pl.semaphore_wait(barrier, count)


class Spread:
    def __init__(self, grid, parts, chain, source_for, out_ref, send_sem, recv_sem, own_sem):
        self.grid, self.source_for, self.out = grid, source_for, out_ref
        self.send_sem, self.recv_sem, self.own_sem = send_sem, recv_sem, own_sem
        self.chain = chain
        self.parts, self.rows = parts, out_ref.shape[1] // parts
        self.sent, self.count, self.maybe = [], [0] * parts, []

    def send(self, part, source, block, peer, when=None):
        slot = self.count[part]
        self.count[part] += 1
        copy = pltpu.make_async_remote_copy(
            src_ref=source.at[pl.ds(part * self.rows, self.rows)],
            dst_ref=self.out.at[block, pl.ds(part * self.rows, self.rows)],
            send_sem=self.send_sem.at[part, slot],
            recv_sem=self.recv_sem.at[part, block],
            device_id={"dp": peer},
            device_id_type=MESH,
        )
        if when is None:
            copy.start()
            self.sent.append(copy)
        else:
            pl.when(when)(copy.start)
            self.maybe.append((when, copy))

    def arrived(self, part, block):
        view = self.out.at[block, pl.ds(part * self.rows, self.rows)]
        pltpu.make_async_copy(view, view, self.recv_sem.at[part, block]).wait()

    def onward(self, part, source, block, near_too):
        grid = self.grid
        far, near, core = grid.here()
        if near_too:
            for k in range(1, grid.near):
                self.send(part, source, block, grid.at(far, (near + k) % grid.near, core))
        self.send(part, source, block, grid.at(far, near, 1 - core))

    def first(self, part):
        grid = self.grid
        far, near, core = grid.here()
        mine = grid.at(far, near, core)
        if self.chain:
            for step in (1, -1):
                to = jnp.clip(far + step, 0, grid.far - 1)
                there = far + step < grid.far if step > 0 else far + step >= 0
                self.send(part, self.source_for(to), mine, grid.at(to, near, core), there)
        else:
            for k in range(1, grid.far):
                to = (far + k) % grid.far
                self.send(part, self.source_for(to), mine, grid.at(to, near, core))
        if part == 0:
            self.own = pltpu.make_async_copy(self.source_for(far), self.out.at[mine], self.own_sem)
            self.own.start()

    def second(self, part):
        grid = self.grid
        far, near, core = grid.here()
        self.onward(part, self.source_for(far), grid.at(far, near, core), True)
        for origin in nearest(far, grid.far):
            block = grid.at(origin, near, core)
            self.arrived(part, block)
            if self.chain:
                to, there = beyond(far, origin, grid.far)
                self.send(part, self.out.at[block], block, grid.at(to, near, core), there)
            self.onward(part, self.out.at[block], block, True)

    def third(self, part):
        grid = self.grid
        far, near, core = grid.here()
        for k in range(1, grid.near):
            for j in range(grid.far):
                block = grid.at((far + grid.far - j) % grid.far, (near + grid.near - k) % grid.near, core)
                self.arrived(part, block)
                self.onward(part, self.out.at[block], block, False)

    def last(self):
        grid = self.grid
        far, near, core = grid.here()
        for part in range(self.parts):
            for j in range(grid.far):
                for k in range(grid.near):
                    self.arrived(part, grid.at((far + j) % grid.far, (near + k) % grid.near, 1 - core))
        for copy in self.sent:
            copy.wait_send()
        for when, copy in self.maybe:
            pl.when(when)(copy.wait_send)
        self.own.wait()

    def run(self):
        for step in range(self.parts + 2):
            if step < self.parts:
                self.first(step)
            if 1 <= step <= self.parts:
                self.second(step - 1)
            if 2 <= step:
                self.third(step - 2)
        self.last()


def share_kernel(grid, block_ref, out_ref, send_sem, recv_sem, own_sem):
    greet(grid, False)
    Spread(grid, TABLE_PARTS, True, lambda to: block_ref, out_ref, send_sem, recv_sem, own_sem).run()


def items_kernel(
    grid, send_ref, base_ref, gain_ref, weight_ref, items_out, weight_out,
    partial_buf, mine_buf, half_send, half_recv, item_send, item_recv, item_own,
    send_sem, recv_sem, own_sem,
):
    far, near, core = grid.here()
    half = lax.axis_index("tp")
    greet(grid, True)
    halves = []
    for k in range(1, grid.halves):
        peer = (half + k) % grid.halves
        copy = pltpu.make_async_remote_copy(
            src_ref=send_ref.at[peer],
            dst_ref=partial_buf.at[k - 1],
            send_sem=half_send.at[k - 1],
            recv_sem=half_recv.at[k - 1],
            device_id={"tp": peer},
            device_id_type=MESH,
        )
        copy.start()
        halves.append(copy)
    spread = Spread(grid, WEIGHT_PARTS, False, lambda to: weight_ref.at[to // grid.share], weight_out, send_sem, recv_sem, own_sem)
    for part in range(WEIGHT_PARTS):
        spread.first(part)
    for copy in halves:
        copy.wait()

    column, rest = far // grid.share, far % grid.share
    parts = mine_buf.shape[0] // ITEM_ROWS
    sent, maybe, count = [], [], [0] * parts

    def send_items(part, source, place, peer, when=None):
        rows = pl.ds(part * ITEM_ROWS, ITEM_ROWS)
        copy = pltpu.make_async_remote_copy(
            src_ref=source.at[rows],
            dst_ref=items_out.at[place, half, rows],
            send_sem=item_send.at[part, count[part]],
            recv_sem=item_recv.at[part, place, half],
            device_id=peer,
            device_id_type=MESH,
        )
        count[part] += 1
        if when is None:
            copy.start()
            sent.append(copy)
        else:
            pl.when(when)(copy.start)
            maybe.append((when, copy))

    def arrived(part, place, origin):
        view = items_out.at[place, origin, pl.ds(part * ITEM_ROWS, ITEM_ROWS)]
        pltpu.make_async_copy(view, view, item_recv.at[part, place, origin]).wait()

    for part in range(parts):
        rows = pl.ds(part * ITEM_ROWS, ITEM_ROWS)
        total = base_ref[rows, :]
        for k in range(1, grid.halves):
            total = total + partial_buf[k - 1, rows, :].astype(jnp.float32)
        vec = total.astype(jnp.bfloat16).astype(jnp.float32)
        scale = lax.rsqrt(jnp.mean(vec * vec, axis=1, keepdims=True) + EPS)
        mine_buf[rows, :] = (vec * scale * gain_ref[...]).astype(jnp.bfloat16)
        for step in (1, -1):
            to = jnp.clip(column + step, 0, grid.splits - 1) * grid.share + rest
            there = column + step < grid.splits if step > 0 else column + step >= 0
            send_items(part, mine_buf, column, {"dp": grid.at(to, near, core)}, there)
        for k in range(1, grid.halves):
            send_items(part, mine_buf, column, {"tp": (half + k) % grid.halves})
    own = pltpu.make_async_copy(mine_buf, items_out.at[column, half], item_own)
    own.start()
    for step in range(max(parts, WEIGHT_PARTS)):
        if step < WEIGHT_PARTS:
            spread.second(step)
        if step < parts:
            for place in nearest(column, grid.splits):
                arrived(step, place, half)
                to, there = beyond(column, place, grid.splits)
                peer = {"dp": grid.at(to * grid.share + rest, near, core)}
                send_items(step, items_out.at[place, half], place, peer, there)
                for k in range(1, grid.halves):
                    send_items(step, items_out.at[place, half], place, {"tp": (half + k) % grid.halves})
        if 1 <= step <= WEIGHT_PARTS:
            spread.third(step - 1)
    if WEIGHT_PARTS >= parts:
        spread.third(WEIGHT_PARTS - 1)
    for part in range(parts):
        for k in range(1, grid.halves):
            for j in range(grid.splits):
                arrived(part, (column + j) % grid.splits, (half + k) % grid.halves)
    for copy in sent:
        copy.wait_send()
    for when, copy in maybe:
        pl.when(when)(copy.wait_send)
    own.wait()
    spread.last()


def spread_sems(grid, parts):
    sends = grid.far + 1 + grid.far * (grid.near - 1) + grid.far * grid.near
    return [
        pltpu.SemaphoreType.DMA((parts, sends)),
        pltpu.SemaphoreType.DMA((parts, grid.blocks)),
        pltpu.SemaphoreType.DMA,
    ]


def per_device(
    item_query,
    item_keys,
    item_values,
    item_out_weight,
    item_residual,
    cite_home,
    cite_row,
    seq_length,
    user_gain,
    user_weight,
):
    devices, halves = lax.axis_size("dp"), lax.axis_size("tp")
    count_items = item_query.shape[0]
    shard_rows, user_heads, triple = user_weight.shape
    grid = Grid(devices, halves, user_heads)
    splits, share, near, far = grid.splits, grid.share, grid.near, grid.far
    columns = user_heads * triple // splits
    width = item_residual.shape[1]
    rows_half = count_items // halves
    half = lax.axis_index("tp")
    any_space = pl.BlockSpec(memory_space=pl.ANY)
    in_vmem = pl.BlockSpec(memory_space=pltpu.VMEM)

    by_column = jnp.swapaxes(user_weight.reshape(shard_rows, splits, columns), 0, 1)
    attended = attend(item_query, item_keys, item_values)
    partial_value = jnp.dot(attended, item_out_weight, preferred_element_type=jnp.float32)
    to_send = partial_value.astype(jnp.bfloat16).reshape(halves, rows_half, width)
    base = lax.dynamic_slice_in_dim(partial_value, half * rows_half, rows_half, 0) + lax.dynamic_slice_in_dim(
        item_residual, half * rows_half, rows_half, 0
    ).astype(jnp.float32)
    sends = splits + 1 + splits * (halves - 1)
    normed, weight = pl.pallas_call(
        functools.partial(items_kernel, grid),
        out_shape=(
            jax.ShapeDtypeStruct((splits, halves, rows_half, width), jnp.bfloat16),
            jax.ShapeDtypeStruct((devices, shard_rows, columns), jnp.bfloat16),
        ),
        in_specs=[any_space, in_vmem, in_vmem, any_space],
        out_specs=(any_space, any_space),
        scratch_shapes=[
            pltpu.VMEM((halves - 1, rows_half, width), jnp.bfloat16),
            pltpu.VMEM((rows_half, width), jnp.bfloat16),
            pltpu.SemaphoreType.DMA((halves - 1,)),
            pltpu.SemaphoreType.DMA((halves - 1,)),
            pltpu.SemaphoreType.DMA((rows_half // ITEM_ROWS, sends)),
            pltpu.SemaphoreType.DMA((rows_half // ITEM_ROWS, splits, halves)),
            pltpu.SemaphoreType.DMA,
        ]
        + spread_sems(grid, WEIGHT_PARTS),
        compiler_params=pltpu.CompilerParams(
            collective_id=0, has_side_effects=True, vmem_limit_bytes=24 << 20
        ),
        name="gather_items",
    )(to_send, base, user_gain[None, :], by_column)

    normed = normed.reshape(splits * count_items, width)
    weight = weight.reshape(devices * shard_rows, columns)
    projected = jnp.dot(normed, weight, preferred_element_type=jnp.float32).astype(jnp.bfloat16)
    table = pl.pallas_call(
        functools.partial(share_kernel, grid),
        out_shape=jax.ShapeDtypeStruct((devices,) + projected.shape, jnp.bfloat16),
        in_specs=[any_space],
        out_specs=any_space,
        scratch_shapes=spread_sems(grid, TABLE_PARTS),
        compiler_params=pltpu.CompilerParams(collective_id=1, has_side_effects=True),
        name="gather_table",
    )(projected)
    table = table.reshape(splits, devices * count_items, columns)

    home = cite_home[:, 0]
    home_far, home_near, home_core = home // (near * CORES), (home // CORES) % near, home % CORES
    block = ((home_far % share) * near + home_near) * CORES + home_core
    place = (block * splits + home_far // share) * count_items + cite_row
    live = jnp.arange(home.shape[0], dtype=jnp.int32) < seq_length[0]
    place = jnp.where(live, place, -1)
    chosen = (place[:, None] == jnp.arange(devices * count_items, dtype=jnp.int32)[None, :]).astype(jnp.bfloat16)
    out = jnp.einsum("rn,snc->rsc", chosen, table, preferred_element_type=jnp.float32).astype(jnp.bfloat16)
    return out.reshape(home.shape[0], user_heads, triple)


def solution(mesh):
    in_specs = (
        P("dp", "tp"),
        P("dp", None, "tp"),
        P("dp", None, "tp"),
        P("tp", None),
        P("dp", None),
        P("dp", None),
        P("dp"),
        P("dp"),
        P(),
        P("dp", "tp", None),
    )
    out_specs = P("dp", "tp", None)
    return jax.shard_map(
        per_device, mesh=mesh, in_specs=in_specs, out_specs=out_specs, check_vma=False
    )
```
